32 devices in a mesh: ctx: 16 (over z, x, core), kvh: 2 (over y).
Axes of the slice: x: 2, y: 2, z: 4, core: 2. Of those that a mesh axis runs over, the one named last changes fastest.
Arguments:
- queries: bfloat16 [8192, 3584], P('ctx', 'kvh'), may hold values from -7.5 to 7.5
- keys: bfloat16 [8192, 512], P('ctx', 'kvh'), may hold values from -6 to 6
- values: bfloat16 [8192, 512], P('ctx', 'kvh'), may hold values from -6 to 6
- columns: int32 [28, 16], P('kvh'), may hold values from 0 to 63, as said below
- offsets: int32 [28, 128], P('kvh'), may hold values from 0 to 511, as said below
- out_weight: bfloat16 [3584, 3584], P('kvh'), may hold values from -0.09375 to 0.09375
Outputs:
- mixed: bfloat16 [8192, 3584], P('ctx', 'kvh')
The draws below stay inside these ranges and needn't reach their ends.
Inputs may be any that keep to these rules, and one draw needn't show every extreme that they name: `columns`: each row lists 16 different blocks of 128 tokens. Rows h with equal h // 7 share a KV head; the union of their lists holds at most 2 blocks among the tokens of any one aligned run of 512 tokens, and exactly 2 among tokens 0 to 511. `offsets`: each row holds 128 different diagonal distances, 0 and 1 among them.
All inputs are finite; a program needn't handle non-finite values.
Results may differ from the reference program's by a relative error of at most 0.012.
Values may be sent and summed in bfloat16 or wider, within the bound.
A program may use at most 320 MiB of HBM per device.

```python
import math
import jax
import jax.numpy as jnp
from jax import lax

D = 3584
QH = 28
KVH = 4
HD = 128
TOK_DEV = 512
BLK = 128
NV = 16
NS = 128
CAP = 2
TOKENS = 8192
WIN = 512


def draw_columns(key, part):
    device_count = TOKENS // TOK_DEV
    per_device = TOK_DEV // BLK
    group_size = QH // KVH
    pool_size = device_count * CAP

    def one_group(group_key):
        cand_key, head_key, sink_key = jax.random.split(group_key, 3)
        picks = jax.vmap(lambda split_key: jax.random.permutation(split_key, per_device)[:CAP])(jax.random.split(cand_key, device_count))
        candidates = (jnp.arange(device_count, dtype=jnp.int32)[:, None] * per_device + picks.astype(jnp.int32)).reshape(-1)
        sink_head = jax.random.randint(sink_key, (), 0, group_size)

        def one_head(split_key, index):
            drawn_key, rest_key, order_key = jax.random.split(split_key, 3)
            drawn = jax.random.permutation(drawn_key, pool_size)[:NV].astype(jnp.int32)
            forced = jnp.concatenate([jnp.arange(CAP, dtype=jnp.int32), jax.random.permutation(rest_key, pool_size - CAP)[:NV - CAP].astype(jnp.int32) + CAP])
            chosen = jnp.where(index == sink_head, forced, drawn)
            chosen = chosen[jax.random.permutation(order_key, NV)]
            return candidates[chosen]
        return jax.vmap(one_head)(jax.random.split(head_key, group_size), jnp.arange(group_size, dtype=jnp.int32))
    lists = jax.vmap(one_group)(jax.random.split(jax.random.fold_in(key, 11), KVH))
    return lists.reshape(QH, NV).astype(jnp.int32)


def draw_offsets(key, part):

    def one_row(split_key):
        first_key, order_key = jax.random.split(split_key)
        others = jax.random.permutation(first_key, WIN - 2)[:NS - 2].astype(jnp.int32) + 2
        row_values = jnp.concatenate([jnp.array([0, 1], jnp.int32), others])
        return row_values[jax.random.permutation(order_key, NS)]
    return jax.vmap(one_row)(jax.random.split(jax.random.fold_in(key, 23), QH)).astype(jnp.int32)


def make_pair(key):
    base_key = jax.random.fold_in(key, 5)
    query_key, key_key = jax.random.split(base_key, 2)
    query_part = jnp.clip(jax.random.normal(query_key, (TOKENS, QH * HD), jnp.float32), -6.0, 6.0)
    key_part = jnp.clip(jax.random.normal(key_key, (TOKENS, KVH * HD), jnp.float32), -6.0, 6.0)
    return (query_part, key_part)


def draw_queries(key, part):
    return make_pair(key)[0].astype(jnp.bfloat16)


def draw_keys(key, part):
    return make_pair(key)[1].astype(jnp.bfloat16)


def levels(key, extent, shards, least, high):
    level, own = 1.0, jax.random.fold_in(key, 6)
    for position, parts in shards:
        draws = jnp.exp(jax.random.uniform(jax.random.fold_in(own, position), (parts,), jnp.float32, least / len(shards), high / len(shards)))
        level = level * jnp.repeat(draws, extent[position] // parts).reshape([-1 if axis == position else 1 for axis in range(len(extent))])
    return level


def normal_values(stream_key, dims, scale, reach, pieces=(), kind=jnp.bfloat16):
    entries = jax.random.normal(stream_key, dims, jnp.float32) * scale
    if len(pieces) > 0:
        entries = levels(stream_key, dims, pieces, -0.22, 0.18) * entries
    return jnp.clip(entries, min=-reach, max=reach).astype(kind)


def setup_inputs(seed: int = 0) -> dict:
    arg_keys = jax.random.split(jax.random.key(seed), 7)
    queries = draw_queries(jax.random.fold_in(arg_keys[6], 71), 0)
    keys = draw_keys(jax.random.fold_in(arg_keys[6], 71), 0)
    values = normal_values(arg_keys[2], (TOKENS, KVH * HD), 1.0, 6.0, ((0, 16), (1, 2)))
    columns = draw_columns(jax.random.fold_in(arg_keys[6], 71), 0)
    offsets = draw_offsets(jax.random.fold_in(arg_keys[6], 71), 0)
    out_weight = normal_values(arg_keys[5], (QH * HD, D), (QH * HD) ** -0.5, 0.09375, ((0, 2),))
    return {"queries": queries, "keys": keys, "values": values, "columns": columns, "offsets": offsets, "out_weight": out_weight}


masked_score = -1e+30

def reference(queries, keys, values, columns, offsets, out_weight):
    total_rows = queries.shape[0]
    block_count = total_rows // TOK_DEV
    group_size = QH // KVH
    score_scale = 1.0 / math.sqrt(HD)
    query_heads = queries.reshape(total_rows, QH, HD).transpose(1, 0, 2)
    key_heads = keys.reshape(total_rows, KVH, HD).transpose(1, 0, 2)
    value_heads = values.reshape(total_rows, KVH, HD).transpose(1, 0, 2)
    block_lane = jnp.arange(BLK, dtype=jnp.int32)
    query_lane = jnp.arange(TOK_DEV, dtype=jnp.int32)
    window_lane = jnp.arange(2 * TOK_DEV, dtype=jnp.int32)
    distances = jnp.arange(WIN, dtype=jnp.int32)
    padding = jnp.zeros((TOK_DEV, HD), keys.dtype)

    def one_head(head):
        kv_index = head // group_size
        key_rows = key_heads[kv_index]
        value_rows = value_heads[kv_index]
        column_pos = (columns[head][:, None] * BLK + block_lane[None, :]).reshape(-1).astype(jnp.int32)
        far_keys = jnp.take(key_rows, column_pos, axis=0)
        far_values = jnp.take(value_rows, column_pos, axis=0)
        listed = jnp.any(offsets[head][:, None] == distances[None, :], axis=0)
        padded_keys = jnp.concatenate([padding, key_rows], axis=0)
        padded_values = jnp.concatenate([padding, value_rows], axis=0)
        query_all = query_heads[head]

        def one_block(block):
            start = (block * TOK_DEV).astype(jnp.int32)
            query_rows = lax.dynamic_slice_in_dim(query_all, start, TOK_DEV, 0)
            near_keys = lax.dynamic_slice_in_dim(padded_keys, start, 2 * TOK_DEV, 0)
            near_values = lax.dynamic_slice_in_dim(padded_values, start, 2 * TOK_DEV, 0)
            query_pos = start + query_lane
            key_pos = start - TOK_DEV + window_lane
            far_scores = jnp.dot(query_rows, far_keys.T, preferred_element_type=jnp.float32) * score_scale
            near_scores = jnp.dot(query_rows, near_keys.T, preferred_element_type=jnp.float32) * score_scale
            far_ok = query_pos[:, None] - column_pos[None, :] >= WIN
            distance = query_pos[:, None] - key_pos[None, :]
            near_ok = (distance >= 0) & (distance < WIN) & (key_pos[None, :] >= 0)
            near_ok = near_ok & jnp.take(listed, jnp.clip(distance, 0, WIN - 1))
            far_scores = jnp.where(far_ok, far_scores, masked_score)
            near_scores = jnp.where(near_ok, near_scores, masked_score)
            row_top = jnp.maximum(lax.optimization_barrier(jnp.max(far_scores, axis=1)), lax.optimization_barrier(jnp.max(near_scores, axis=1)))
            far_exp = jnp.exp(far_scores - row_top[:, None])
            near_exp = jnp.exp(near_scores - row_top[:, None])
            row_total = lax.optimization_barrier(jnp.sum(far_exp, axis=1)) + lax.optimization_barrier(jnp.sum(near_exp, axis=1))
            far_weight = (far_exp / row_total[:, None]).astype(jnp.bfloat16)
            near_weight = (near_exp / row_total[:, None]).astype(jnp.bfloat16)
            result = jnp.dot(far_weight, far_values, preferred_element_type=jnp.float32)
            result = result + jnp.dot(near_weight, near_values, preferred_element_type=jnp.float32)
            return result.astype(jnp.bfloat16)
        return lax.map(one_block, jnp.arange(block_count, dtype=jnp.int32))
    head_outputs = lax.map(one_head, jnp.arange(QH, dtype=jnp.int32))
    attended = head_outputs.reshape(QH, total_rows, HD).transpose(1, 0, 2).reshape(total_rows, QH * HD)
    return jnp.dot(attended, out_weight, preferred_element_type=jnp.float32).astype(jnp.bfloat16)
```

```python
import functools
import math

import jax
import jax.numpy as jnp
from jax import lax
from jax.experimental import pallas as pl
from jax.experimental.pallas import tpu as pltpu
from jax.sharding import PartitionSpec as P

HD = 128
BLK = 128
NV = 16
CAP = 2
WIN = 512
WB = WIN // BLK
NEAR = WIN + BLK
PARTS = 2
PAIR = 2
EXP2_SCALE = math.log2(math.e) / math.sqrt(HD)

masked_score = -1e30


def shifted(value, axis, by):
    devices = lax.axis_size(axis)
    pairs = [(i, i + by) for i in range(devices) if 0 <= i + by < devices]
    return lax.ppermute(value, axis, pairs)


def pack_kernel(picked_ref, key_ref, value_ref, out_ref):
    out_ref[0, :, :HD] = key_ref[...]
    out_ref[0, :, HD:] = value_ref[...]


def pack_blocks(keys, values, picked, kv_heads):
    def source(kv, slot, picked_ref):
        return picked_ref[kv * CAP + slot], kv

    return pl.pallas_call(
        pack_kernel,
        grid_spec=pltpu.PrefetchScalarGridSpec(
            num_scalar_prefetch=1,
            grid=(kv_heads, CAP),
            in_specs=[pl.BlockSpec((BLK, HD), source), pl.BlockSpec((BLK, HD), source)],
            out_specs=pl.BlockSpec((1, BLK, 2 * HD), lambda kv, slot, _: (kv, slot, 0)),
        ),
        out_shape=jax.ShapeDtypeStruct((kv_heads, CAP * BLK, 2 * HD), keys.dtype),
    )(picked.reshape(-1), keys, values)


def attend_kernel(
    part, chunks, group_size,
    columns_ref, rank_ref, query_ref, band_ref, pool_ref,
    earlier_keys_ref, keys_ref, earlier_values_ref, values_ref,
    out_ref,
    window_k, window_v, far_k, far_v, far_s, near_s, far_p, near_p,
):
    step = pl.program_id(0)
    shard = lax.axis_index("ctx")
    kv_heads = window_k.shape[0]
    block_count = pool_ref.shape[0] * WB
    first = part * chunks

    @pl.when(step == 0)
    def _():
        ones = jnp.ones((2 * WIN, HD), jnp.bfloat16)
        for kv in range(kv_heads):
            lanes = slice(kv * HD, (kv + 1) * HD)
            window_k[kv, :WIN] = earlier_keys_ref[:, lanes]
            window_k[kv, WIN:] = keys_ref[:, lanes]
            window_v[kv, :WIN, :HD] = earlier_values_ref[:, lanes]
            window_v[kv, WIN:, :HD] = values_ref[:, lanes]
            window_v[kv, :, HD:] = ones
        for pair in range(PAIR):
            far_v[pair, :, HD:] = jnp.ones((NV * BLK, HD), jnp.bfloat16)

    before = jnp.where(shard == 0, masked_score, 0.0).astype(jnp.float32)
    row_lane = lax.broadcasted_iota(jnp.int32, (BLK, BLK), 0)
    key_lane = lax.broadcasted_iota(jnp.int32, (BLK, BLK), 1)
    lower = row_lane >= key_lane

    tops = []
    for pair in range(PAIR):
        head = step * PAIR + pair
        kv = head // group_size
        query = query_ref[:, pair * HD : (pair + 1) * HD]
        blocks = []
        for n in range(NV):
            block = columns_ref[head * NV + n]
            blocks.append(block)
            rank = rank_ref[kv * block_count + block]
            rows = pl.ds(pl.multiple_of(rank * BLK, BLK), BLK)
            far_k[pair, n * BLK : (n + 1) * BLK] = pool_ref[block // WB, kv, rows, :HD]
            far_v[pair, n * BLK : (n + 1) * BLK, :HD] = pool_ref[block // WB, kv, rows, HD:]
        band = pltpu.roll(
            jnp.broadcast_to(band_ref[pair], (BLK, NEAR + BLK)), 0, 1, stride=1, stride_axis=0
        )[:, :NEAR]
        peak = [None] * chunks
        for a in range(chunks):
            rows = slice(a * BLK, (a + 1) * BLK)
            scores = lax.dot_general(
                query[rows],
                window_k[kv, (first + a) * BLK : (first + a) * BLK + NEAR],
                (((1,), (1,)), ((), ())),
                preferred_element_type=jnp.float32,
            )
            oldest = (shard - 1) * WB + first + a
            hit = blocks[0] == oldest
            for n in range(1, NV):
                hit = hit | (blocks[n] == oldest)
            extra = jnp.where(hit, 0.0, masked_score).astype(jnp.float32)
            for t in range(WB + 1):
                lanes = slice(t * BLK, (t + 1) * BLK)
                mask = band[:, lanes]
                if t == 0:
                    mask = jnp.where(lower, extra, mask)
                if first + a + t < WB:
                    mask = mask + before
                tile = scores[:, lanes] + mask
                near_s[pair, rows, lanes] = tile
                peak[a] = tile if peak[a] is None else jnp.maximum(peak[a], tile)
        wide = 4
        for j in range(NV // wide):
            scores = lax.dot_general(
                query,
                far_k[pair, j * wide * BLK : (j + 1) * wide * BLK],
                (((1,), (1,)), ((), ())),
                preferred_element_type=jnp.float32,
            )
            for a in range(chunks):
                rows = slice(a * BLK, (a + 1) * BLK)
                for t in range(wide):
                    n = j * wide + t
                    old = blocks[n] < (shard - 1) * WB + first + a
                    bias = jnp.where(old, 0.0, masked_score).astype(jnp.float32)
                    tile = scores[rows, t * BLK : (t + 1) * BLK] + bias
                    far_s[pair, rows, n * BLK : (n + 1) * BLK] = tile
                    peak[a] = jnp.maximum(peak[a], tile)
        tops.append([jnp.max(peak[a], axis=1, keepdims=True) for a in range(chunks)])

    for pair in range(PAIR):
        head = step * PAIR + pair
        kv = head // group_size
        for a in range(chunks):
            rows = slice(a * BLK, (a + 1) * BLK)
            top = jnp.broadcast_to(tops[pair][a], (BLK, BLK))
            for t in range(WB + 1):
                lanes = slice(t * BLK, (t + 1) * BLK)
                near_p[pair, rows, lanes] = jnp.exp2(
                    (near_s[pair, rows, lanes] - top) * EXP2_SCALE
                ).astype(jnp.bfloat16)
            for n in range(NV):
                lanes = slice(n * BLK, (n + 1) * BLK)
                far_p[pair, rows, lanes] = jnp.exp2(
                    (far_s[pair, rows, lanes] - top) * EXP2_SCALE
                ).astype(jnp.bfloat16)
        total = jnp.dot(far_p[pair], far_v[pair], preferred_element_type=jnp.float32)
        for a in range(chunks):
            rows = slice(a * BLK, (a + 1) * BLK)
            sums = total[rows] + jnp.dot(
                near_p[pair, rows],
                window_v[kv, (first + a) * BLK : (first + a) * BLK + NEAR],
                preferred_element_type=jnp.float32,
            )
            out_ref[rows, pair * HD : (pair + 1) * HD] = (
                sums[:, :HD] / sums[:, HD:]
            ).astype(jnp.bfloat16)


def attend(part, queries, band, pool, columns, rank, earlier_keys, keys, earlier_values, values):
    shard_rows, width = queries.shape
    rows = shard_rows // PARTS
    chunks = rows // BLK
    local_heads = width // HD
    kv_heads = keys.shape[1] // HD
    whole = pl.BlockSpec(memory_space=pltpu.VMEM)
    return pl.pallas_call(
        functools.partial(attend_kernel, part, chunks, local_heads // kv_heads),
        grid_spec=pltpu.PrefetchScalarGridSpec(
            num_scalar_prefetch=2,
            grid=(local_heads // PAIR,),
            in_specs=[
                pl.BlockSpec((rows, PAIR * HD), lambda k, *_: (part, k)),
                pl.BlockSpec((PAIR, 1, NEAR + BLK), lambda k, *_: (k, 0, 0)),
                whole, whole, whole, whole, whole,
            ],
            out_specs=pl.BlockSpec((rows, PAIR * HD), lambda k, *_: (0, k)),
            scratch_shapes=[
                pltpu.VMEM((kv_heads, 2 * WIN, HD), jnp.bfloat16),
                pltpu.VMEM((kv_heads, 2 * WIN, 2 * HD), jnp.bfloat16),
                pltpu.VMEM((PAIR, NV * BLK, HD), jnp.bfloat16),
                pltpu.VMEM((PAIR, NV * BLK, 2 * HD), jnp.bfloat16),
                pltpu.VMEM((PAIR, rows, NV * BLK), jnp.float32),
                pltpu.VMEM((PAIR, rows, NEAR), jnp.float32),
                pltpu.VMEM((PAIR, rows, NV * BLK), jnp.bfloat16),
                pltpu.VMEM((PAIR, rows, NEAR), jnp.bfloat16),
            ],
        ),
        out_shape=jax.ShapeDtypeStruct((rows, width), jnp.bfloat16),
        compiler_params=pltpu.CompilerParams(vmem_limit_bytes=56 * 1024 * 1024),
        cost_estimate=pl.CostEstimate(
            flops=4 * rows * (NV * BLK + NEAR) * width,
            bytes_accessed=2 * pool.size + 4 * rows * width,
            transcendentals=rows * (NV * BLK + NEAR) * local_heads,
        ),
    )(columns.reshape(-1), rank.reshape(-1), queries, band, pool,
      earlier_keys, keys, earlier_values, values)


def shards(queries, keys, values, columns, offsets, out_weight):
    shard_rows = queries.shape[0]
    kv_heads = keys.shape[1] // HD
    owned = shard_rows // BLK
    shard_count = lax.axis_size("ctx")
    shard_index = lax.axis_index("ctx")
    earlier_keys, earlier_values = shifted((keys, values), "ctx", 1)

    block_lane = jnp.arange(shard_count * owned, dtype=jnp.int32)
    listed = jnp.any(
        columns.reshape(kv_heads, -1)[:, :, None] == block_lane[None, None, :], axis=1
    ).astype(jnp.int32).reshape(kv_heads, shard_count, owned)
    earlier = jnp.arange(owned)[:, None] < jnp.arange(owned)[None, :]
    rank = jnp.sum(listed[:, :, :, None] * earlier[None, None].astype(jnp.int32), axis=2)
    own_listed = lax.dynamic_index_in_dim(listed, shard_index, 1, keepdims=False)
    own_rank = lax.dynamic_index_in_dim(rank, shard_index, 1, keepdims=False)
    slot_lane = jnp.arange(CAP, dtype=jnp.int32)
    chosen = (own_listed[:, None, :] > 0) & (own_rank[:, None, :] == slot_lane[None, :, None])
    picked = jnp.sum(
        jnp.where(chosen, jnp.arange(owned, dtype=jnp.int32)[None, None, :], 0), axis=2
    )
    pool = lax.all_gather(pack_blocks(keys, values, picked, kv_heads), "ctx", axis=0)

    distance = WIN - jnp.arange(NEAR + BLK, dtype=jnp.int32)
    band = jnp.where(
        jnp.any(offsets[:, :, None] == distance[None, None, :], axis=1), 0.0, masked_score
    ).astype(jnp.float32)[:, None, :]

    half = out_weight.shape[1] // 2
    upper = lax.axis_index("kvh") == 1
    results = []
    for part in range(PARTS):
        attended = attend(
            part, queries, band, pool, columns, rank,
            earlier_keys, keys, earlier_values, values,
        )
        mixed = jnp.dot(attended, out_weight, preferred_element_type=jnp.float32)
        low, high = mixed[:, :half], mixed[:, half:]
        away = jnp.where(upper, low, high).astype(jnp.bfloat16)
        home = jnp.where(upper, high, low)
        arrived = lax.ppermute(away, "kvh", [(0, 1), (1, 0)])
        results.append((home + arrived.astype(jnp.float32)).astype(jnp.bfloat16))
    return jnp.concatenate(results, axis=0)


def solution(mesh):
    placed = (
        P("ctx", "kvh"),
        P("ctx", "kvh"),
        P("ctx", "kvh"),
        P("kvh", None),
        P("kvh", None),
        P("kvh", None),
    )
    return jax.shard_map(
        shards, mesh=mesh, in_specs=placed, out_specs=P("ctx", "kvh"), check_vma=False
    )
```

```python
import functools
import math

import jax
import jax.numpy as jnp
from jax import lax
from jax.experimental import pallas as pl
from jax.experimental.pallas import tpu as pltpu
from jax.sharding import PartitionSpec as P

HD = 128
BLK = 128
NV = 16
CAP = 2
WIN = 512
WB = WIN // BLK
NEAR = WIN + BLK
PARTS = (2, 1, 1)
LANES = 4
UP, SIDE, PAIRED, DIAGONAL = range(4)
PAIR = 2
EXP2_SCALE = math.log2(math.e) / math.sqrt(HD)

masked_score = -1e30


def gather_kernel(
    shard_count, picked_ref, keys_ref, values_ref,
    pool_ref, earlier_keys_ref, earlier_values_ref,
    packed, send, recv, window_send, window_recv, local,
):
    planes = shard_count // LANES
    me = lax.axis_index("ctx")
    plane, lane = lax.div(me, LANES), lax.rem(me, LANES)
    other_lane = lax.rem(lane + 2, LANES)
    across = plane * LANES + other_lane
    twin = me + 1 - 2 * lax.rem(me, 2)
    mesh_id = pl.DeviceIdType.MESH
    below, above = plane > 0, plane < planes - 1
    has_earlier, has_later = me > 0, me < shard_count - 1

    barrier = pltpu.get_barrier_semaphore()

    def greet(to):
        pl.semaphore_signal(barrier, inc=1, device_id={"ctx": to}, device_id_type=mesh_id)

    greet(across)
    greet(twin)
    beyond = me - 1 + 2 * lax.rem(me, 2)
    has_beyond = (beyond >= 0) & (beyond < shard_count)
    for there, to in ((below, me - LANES), (above, me + LANES), (has_beyond, beyond)):
        pl.when(there)(functools.partial(greet, to))
    kv_heads = packed.shape[0]
    for kv in range(kv_heads):
        lanes = slice(kv * HD, (kv + 1) * HD)
        for slot in range(CAP):
            chosen = jnp.full((BLK, HD), picked_ref[kv * CAP + slot], jnp.int32)
            out = slice(slot * BLK, (slot + 1) * BLK)
            for ref, start in ((keys_ref, 0), (values_ref, HD)):
                tile = ref[:BLK, lanes].astype(jnp.float32)
                for block in range(1, ref.shape[0] // BLK):
                    own_tile = ref[block * BLK : (block + 1) * BLK, lanes].astype(jnp.float32)
                    tile = jnp.where(chosen == block, own_tile, tile)
                packed[kv, out, start : start + HD] = tile.astype(packed.dtype)
    peers = jnp.int32(2)
    for there in (below, above, has_beyond):
        peers = peers + jnp.where(there, 1, 0).astype(jnp.int32)
    pl.semaphore_wait(barrier, peers)

    def move(kind, k, slot, to, arrival):
        source = packed if k == 0 and kind != DIAGONAL else pool_ref.at[slot]
        return pltpu.make_async_remote_copy(
            src_ref=source, dst_ref=pool_ref.at[slot],
            send_sem=send.at[kind, k], recv_sem=recv.at[kind, arrival],
            device_id={"ctx": to}, device_id_type=mesh_id,
        )

    def up(k):
        return move(UP, k, (plane - k) * LANES + lane, me + LANES, k + 1)

    def side(k):
        return move(SIDE, k, (plane - k) * LANES + lane, across, k)

    def pair(k):
        return move(PAIRED, k, (plane - k) * LANES + lane, twin, k)

    def diagonal(k):
        return move(DIAGONAL, k, (plane - k) * LANES + other_lane, twin, k)

    def window(i):
        source, target = ((keys_ref, earlier_keys_ref), (values_ref, earlier_values_ref))[i]
        return pltpu.make_async_remote_copy(
            src_ref=source, dst_ref=target,
            send_sem=window_send.at[i], recv_sem=window_recv.at[i],
            device_id={"ctx": me + 1}, device_id_type=mesh_id,
        )

    def arrived(kind, k, from_lane):
        slot = (plane - k) * LANES + from_lane
        pltpu.make_async_remote_copy(
            src_ref=packed, dst_ref=pool_ref.at[slot],
            send_sem=send.at[kind, k], recv_sem=recv.at[kind, k],
            device_id={"ctx": twin}, device_id_type=mesh_id,
        ).wait_recv()

    twin_lane = lane + 1 - 2 * lax.rem(me, 2)
    own = pltpu.make_async_copy(packed, pool_ref.at[me], local.at[0])
    own.start()

    fill = [
        pltpu.make_async_copy(keys_ref, earlier_keys_ref, local.at[1]),
        pltpu.make_async_copy(values_ref, earlier_values_ref, local.at[2]),
    ]

    @pl.when(jnp.logical_not(has_earlier))
    def _():
        for copy in fill:
            copy.start()
        for copy in fill:
            copy.wait()

    def stage(k):
        if k > 0:
            arrived(UP, k, lane)
        pl.when(above)(lambda: up(k).start()) if k < planes - 1 else None
        side(k).start()
        pair(k).start()

    def forward(k):
        arrived(SIDE, k, other_lane)
        diagonal(k).start()

    for k in range(planes):
        pl.when(plane >= k)(functools.partial(stage, k))
        if k == 0:

            @pl.when(has_later)
            def _():
                window(0).start()
                window(1).start()

        else:
            pl.when(plane >= k - 1)(functools.partial(forward, k - 1))
    pl.when(plane >= planes - 1)(functools.partial(forward, planes - 1))

    def finish(k):
        arrived(PAIRED, k, twin_lane)
        arrived(DIAGONAL, k, lax.rem(twin_lane + 2, LANES))
        side(k).wait_send()
        pair(k).wait_send()
        diagonal(k).wait_send()
        if k < planes - 1:
            pl.when(above)(lambda: up(k).wait_send())

    for k in range(planes):
        pl.when(plane >= k)(functools.partial(finish, k))
    own.wait()

    @pl.when(has_earlier)
    def _():
        window(0).wait_recv()
        window(1).wait_recv()

    @pl.when(has_later)
    def _():
        window(0).wait_send()
        window(1).wait_send()


def gather(picked, keys, values):
    shard_count = lax.axis_size("ctx")
    planes = shard_count // LANES
    kv_heads = keys.shape[1] // HD
    whole = pl.BlockSpec(memory_space=pltpu.VMEM)
    anywhere = pl.BlockSpec(memory_space=pl.ANY)
    block = (kv_heads, CAP * BLK, 2 * HD)
    return pl.pallas_call(
        functools.partial(gather_kernel, shard_count),
        out_shape=[
            jax.ShapeDtypeStruct((shard_count,) + block, keys.dtype),
            jax.ShapeDtypeStruct(keys.shape, keys.dtype),
            jax.ShapeDtypeStruct(values.shape, values.dtype),
        ],
        in_specs=[pl.BlockSpec(memory_space=pltpu.SMEM), whole, whole],
        out_specs=[anywhere, anywhere, anywhere],
        scratch_shapes=[
            pltpu.VMEM(block, keys.dtype),
            pltpu.SemaphoreType.DMA((4, planes)),
            pltpu.SemaphoreType.DMA((4, planes)),
            pltpu.SemaphoreType.DMA((2,)),
            pltpu.SemaphoreType.DMA((2,)),
            pltpu.SemaphoreType.DMA((3,)),
        ],
        compiler_params=pltpu.CompilerParams(collective_id=0, has_side_effects=True),
    )(picked.reshape(-1), keys, values)


def attend_kernel(
    first, chunks, group_size,
    columns_ref, rank_ref, query_ref, band_ref, pool_ref,
    earlier_keys_ref, keys_ref, earlier_values_ref, values_ref,
    out_ref,
    window_k, window_v, far_k, far_v, far_s, near_s, far_p, near_p,
):
    step = pl.program_id(0)
    shard = lax.axis_index("ctx")
    kv_heads = window_k.shape[0]
    block_count = pool_ref.shape[0] * WB

    @pl.when(step == 0)
    def _():
        ones = jnp.ones((2 * WIN, HD), jnp.bfloat16)
        for kv in range(kv_heads):
            lanes = slice(kv * HD, (kv + 1) * HD)
            window_k[kv, :WIN] = earlier_keys_ref[:, lanes]
            window_k[kv, WIN:] = keys_ref[:, lanes]
            window_v[kv, :WIN, :HD] = earlier_values_ref[:, lanes]
            window_v[kv, WIN:, :HD] = values_ref[:, lanes]
            window_v[kv, :, HD:] = ones
        for pair in range(PAIR):
            far_v[pair, :, HD:] = jnp.ones((NV * BLK, HD), jnp.bfloat16)

    before = jnp.where(shard == 0, masked_score, 0.0).astype(jnp.float32)
    row_lane = lax.broadcasted_iota(jnp.int32, (BLK, BLK), 0)
    key_lane = lax.broadcasted_iota(jnp.int32, (BLK, BLK), 1)
    lower = row_lane >= key_lane

    tops = []
    for pair in range(PAIR):
        head = step * PAIR + pair
        kv = head // group_size
        query = query_ref[:, pair * HD : (pair + 1) * HD]
        blocks = []
        for n in range(NV):
            block = columns_ref[head * NV + n]
            blocks.append(block)
            source = jnp.minimum(block // WB, shard)
            rank = jnp.minimum(rank_ref[kv * block_count + block], CAP - 1)
            rows = pl.ds(pl.multiple_of(rank * BLK, BLK), BLK)
            far_k[pair, n * BLK : (n + 1) * BLK] = pool_ref[source, kv, rows, :HD]
            far_v[pair, n * BLK : (n + 1) * BLK, :HD] = pool_ref[source, kv, rows, HD:]
        band = pltpu.roll(
            jnp.broadcast_to(band_ref[pair], (BLK, NEAR + BLK)), 0, 1, stride=1, stride_axis=0
        )[:, :NEAR]
        peak = [None] * chunks
        for a in range(chunks):
            rows = slice(a * BLK, (a + 1) * BLK)
            scores = lax.dot_general(
                query[rows],
                window_k[kv, (first + a) * BLK : (first + a) * BLK + NEAR],
                (((1,), (1,)), ((), ())),
                preferred_element_type=jnp.float32,
            )
            oldest = (shard - 1) * WB + first + a
            hit = blocks[0] == oldest
            for n in range(1, NV):
                hit = hit | (blocks[n] == oldest)
            extra = jnp.where(hit, 0.0, masked_score).astype(jnp.float32)
            for t in range(WB + 1):
                lanes = slice(t * BLK, (t + 1) * BLK)
                mask = band[:, lanes]
                if t == 0:
                    mask = jnp.where(lower, extra, mask)
                if first + a + t < WB:
                    mask = mask + before
                tile = scores[:, lanes] + mask
                near_s[pair, rows, lanes] = tile
                peak[a] = tile if peak[a] is None else jnp.maximum(peak[a], tile)
        wide = 4
        for j in range(NV // wide):
            scores = lax.dot_general(
                query,
                far_k[pair, j * wide * BLK : (j + 1) * wide * BLK],
                (((1,), (1,)), ((), ())),
                preferred_element_type=jnp.float32,
            )
            for a in range(chunks):
                rows = slice(a * BLK, (a + 1) * BLK)
                for t in range(wide):
                    n = j * wide + t
                    old = blocks[n] < (shard - 1) * WB + first + a
                    bias = jnp.where(old, 0.0, masked_score).astype(jnp.float32)
                    tile = scores[rows, t * BLK : (t + 1) * BLK] + bias
                    far_s[pair, rows, n * BLK : (n + 1) * BLK] = tile
                    peak[a] = jnp.maximum(peak[a], tile)
        tops.append([jnp.max(peak[a], axis=1, keepdims=True) for a in range(chunks)])

    for pair in range(PAIR):
        head = step * PAIR + pair
        kv = head // group_size
        for a in range(chunks):
            rows = slice(a * BLK, (a + 1) * BLK)
            top = jnp.broadcast_to(tops[pair][a], (BLK, BLK))
            for t in range(WB + 1):
                lanes = slice(t * BLK, (t + 1) * BLK)
                near_p[pair, rows, lanes] = jnp.exp2(
                    (near_s[pair, rows, lanes] - top) * EXP2_SCALE
                ).astype(jnp.bfloat16)
            for n in range(NV):
                lanes = slice(n * BLK, (n + 1) * BLK)
                far_p[pair, rows, lanes] = jnp.exp2(
                    (far_s[pair, rows, lanes] - top) * EXP2_SCALE
                ).astype(jnp.bfloat16)
        total = jnp.dot(far_p[pair], far_v[pair], preferred_element_type=jnp.float32)
        for a in range(chunks):
            rows = slice(a * BLK, (a + 1) * BLK)
            sums = total[rows] + jnp.dot(
                near_p[pair, rows],
                window_v[kv, (first + a) * BLK : (first + a) * BLK + NEAR],
                preferred_element_type=jnp.float32,
            )
            out_ref[rows, pair * HD : (pair + 1) * HD] = (
                sums[:, :HD] / sums[:, HD:]
            ).astype(jnp.bfloat16)


def attend(first, chunks, queries, band, pool, columns, rank, earlier_keys, keys, earlier_values, values):
    width = queries.shape[1]
    rows = chunks * BLK
    local_heads = width // HD
    kv_heads = keys.shape[1] // HD
    whole = pl.BlockSpec(memory_space=pltpu.VMEM)
    return pl.pallas_call(
        functools.partial(attend_kernel, first, chunks, local_heads // kv_heads),
        grid_spec=pltpu.PrefetchScalarGridSpec(
            num_scalar_prefetch=2,
            grid=(local_heads // PAIR,),
            in_specs=[
                pl.BlockSpec((rows, PAIR * HD), lambda k, *_: (first // chunks, k)),
                pl.BlockSpec((PAIR, 1, NEAR + BLK), lambda k, *_: (k, 0, 0)),
                whole, whole, whole, whole, whole,
            ],
            out_specs=pl.BlockSpec((rows, PAIR * HD), lambda k, *_: (0, k)),
            scratch_shapes=[
                pltpu.VMEM((kv_heads, 2 * WIN, HD), jnp.bfloat16),
                pltpu.VMEM((kv_heads, 2 * WIN, 2 * HD), jnp.bfloat16),
                pltpu.VMEM((PAIR, NV * BLK, HD), jnp.bfloat16),
                pltpu.VMEM((PAIR, NV * BLK, 2 * HD), jnp.bfloat16),
                pltpu.VMEM((PAIR, rows, NV * BLK), jnp.float32),
                pltpu.VMEM((PAIR, rows, NEAR), jnp.float32),
                pltpu.VMEM((PAIR, rows, NV * BLK), jnp.bfloat16),
                pltpu.VMEM((PAIR, rows, NEAR), jnp.bfloat16),
            ],
        ),
        out_shape=jax.ShapeDtypeStruct((rows, width), jnp.bfloat16),
        compiler_params=pltpu.CompilerParams(vmem_limit_bytes=56 * 1024 * 1024),
        cost_estimate=pl.CostEstimate(
            flops=4 * rows * (NV * BLK + NEAR) * width,
            bytes_accessed=2 * pool.size + 4 * rows * width,
            transcendentals=rows * (NV * BLK + NEAR) * local_heads,
        ),
    )(columns.reshape(-1), rank.reshape(-1), queries, band, pool,
      earlier_keys, keys, earlier_values, values)


def shards(queries, keys, values, columns, offsets, out_weight):
    shard_rows = queries.shape[0]
    kv_heads = keys.shape[1] // HD
    owned = shard_rows // BLK
    shard_count = lax.axis_size("ctx")
    shard_index = lax.axis_index("ctx")

    block_lane = jnp.arange(shard_count * owned, dtype=jnp.int32)
    listed = jnp.any(
        columns.reshape(kv_heads, -1)[:, :, None] == block_lane[None, None, :], axis=1
    ).astype(jnp.int32).reshape(kv_heads, shard_count, owned)
    earlier = jnp.arange(owned)[:, None] < jnp.arange(owned)[None, :]
    rank = jnp.sum(listed[:, :, :, None] * earlier[None, None].astype(jnp.int32), axis=2)
    own_listed = lax.dynamic_index_in_dim(listed, shard_index, 1, keepdims=False)
    own_rank = lax.dynamic_index_in_dim(rank, shard_index, 1, keepdims=False)
    slot_lane = jnp.arange(CAP, dtype=jnp.int32)
    chosen = (own_listed[:, None, :] > 0) & (own_rank[:, None, :] == slot_lane[None, :, None])
    picked = jnp.sum(
        jnp.where(chosen, jnp.arange(owned, dtype=jnp.int32)[None, None, :], 0), axis=2
    )
    pool, earlier_keys, earlier_values = gather(picked, keys, values)

    distance = WIN - jnp.arange(NEAR + BLK, dtype=jnp.int32)
    band = jnp.where(
        jnp.any(offsets[:, :, None] == distance[None, None, :], axis=1), 0.0, masked_score
    ).astype(jnp.float32)[:, None, :]

    half = out_weight.shape[1] // 2
    upper = lax.axis_index("kvh") == 1
    results = []
    first = 0
    for chunks in PARTS:
        attended = attend(
            first, chunks, queries, band, pool, columns, rank,
            earlier_keys, keys, earlier_values, values,
        )
        mixed = jnp.dot(attended, out_weight, preferred_element_type=jnp.float32)
        low, high = mixed[:, :half], mixed[:, half:]
        away = jnp.where(upper, low, high).astype(jnp.bfloat16)
        home = jnp.where(upper, high, low)
        arrived = lax.ppermute(away, "kvh", [(0, 1), (1, 0)])
        first += chunks
        results.append((home + arrived.astype(jnp.float32)).astype(jnp.bfloat16))
    return jnp.concatenate(results, axis=0)


def solution(mesh):
    placed = (
        P("ctx", "kvh"),
        P("ctx", "kvh"),
        P("ctx", "kvh"),
        P("kvh", None),
        P("kvh", None),
        P("kvh", None),
    )
    return jax.shard_map(
        shards, mesh=mesh, in_specs=placed, out_specs=P("ctx", "kvh"), check_vma=False
    )
```

```python
import functools
import math

import jax
import jax.numpy as jnp
from jax import lax
from jax.experimental import pallas as pl
from jax.experimental.pallas import tpu as pltpu
from jax.sharding import PartitionSpec as P

HD = 128
BLK = 128
NV = 16
CAP = 2
WIN = 512
WB = WIN // BLK
NEAR = WIN + BLK
PARTS = (2, 2)
LANES = 4
UP, SIDE, PAIRED, DIAGONAL = range(4)
PAIR = 2
EXP2_SCALE = math.log2(math.e) / math.sqrt(HD)

masked_score = -1e30


def gather_kernel(
    shard_count, picked_ref, keys_ref, values_ref,
    pool_ref, earlier_keys_ref, earlier_values_ref,
    packed, send, recv, window_send, window_recv, local,
):
    planes = shard_count // LANES
    me = lax.axis_index("ctx")
    plane, lane = lax.div(me, LANES), lax.rem(me, LANES)
    other_lane = lax.rem(lane + 2, LANES)
    across = plane * LANES + other_lane
    twin = me + 1 - 2 * lax.rem(me, 2)
    mesh_id = pl.DeviceIdType.MESH
    below, above = plane > 0, plane < planes - 1
    has_earlier, has_later = me > 0, me < shard_count - 1

    barrier = pltpu.get_barrier_semaphore()

    def greet(to):
        pl.semaphore_signal(barrier, inc=1, device_id={"ctx": to}, device_id_type=mesh_id)

    greet(across)
    greet(twin)
    beyond = me - 1 + 2 * lax.rem(me, 2)
    has_beyond = (beyond >= 0) & (beyond < shard_count)
    for there, to in ((below, me - LANES), (above, me + LANES), (has_beyond, beyond)):
        pl.when(there)(functools.partial(greet, to))
    kv_heads = packed.shape[0]
    for kv in range(kv_heads):
        lanes = slice(kv * HD, (kv + 1) * HD)
        for slot in range(CAP):
            chosen = jnp.full((BLK, HD), picked_ref[kv * CAP + slot], jnp.int32)
            out = slice(slot * BLK, (slot + 1) * BLK)
            for ref, start in ((keys_ref, 0), (values_ref, HD)):
                tile = ref[:BLK, lanes].astype(jnp.float32)
                for block in range(1, ref.shape[0] // BLK):
                    own_tile = ref[block * BLK : (block + 1) * BLK, lanes].astype(jnp.float32)
                    tile = jnp.where(chosen == block, own_tile, tile)
                packed[kv, out, start : start + HD] = tile.astype(packed.dtype)
    peers = jnp.int32(2)
    for there in (below, above, has_beyond):
        peers = peers + jnp.where(there, 1, 0).astype(jnp.int32)
    pl.semaphore_wait(barrier, peers)

    def move(kind, k, slot, to, arrival):
        source = packed if k == 0 and kind != DIAGONAL else pool_ref.at[slot]
        return pltpu.make_async_remote_copy(
            src_ref=source, dst_ref=pool_ref.at[slot],
            send_sem=send.at[kind, k], recv_sem=recv.at[kind, arrival],
            device_id={"ctx": to}, device_id_type=mesh_id,
        )

    def up(k):
        return move(UP, k, (plane - k) * LANES + lane, me + LANES, k + 1)

    def side(k):
        return move(SIDE, k, (plane - k) * LANES + lane, across, k)

    def pair(k):
        return move(PAIRED, k, (plane - k) * LANES + lane, twin, k)

    def diagonal(k):
        return move(DIAGONAL, k, (plane - k) * LANES + other_lane, twin, k)

    def window(i):
        source, target = ((keys_ref, earlier_keys_ref), (values_ref, earlier_values_ref))[i]
        return pltpu.make_async_remote_copy(
            src_ref=source, dst_ref=target,
            send_sem=window_send.at[i], recv_sem=window_recv.at[i],
            device_id={"ctx": me + 1}, device_id_type=mesh_id,
        )

    def arrived(kind, k, from_lane):
        slot = (plane - k) * LANES + from_lane
        pltpu.make_async_remote_copy(
            src_ref=packed, dst_ref=pool_ref.at[slot],
            send_sem=send.at[kind, k], recv_sem=recv.at[kind, k],
            device_id={"ctx": twin}, device_id_type=mesh_id,
        ).wait_recv()

    twin_lane = lane + 1 - 2 * lax.rem(me, 2)
    own = pltpu.make_async_copy(packed, pool_ref.at[me], local.at[0])
    own.start()

    fill = [
        pltpu.make_async_copy(keys_ref, earlier_keys_ref, local.at[1]),
        pltpu.make_async_copy(values_ref, earlier_values_ref, local.at[2]),
    ]

    @pl.when(jnp.logical_not(has_earlier))
    def _():
        for copy in fill:
            copy.start()
        for copy in fill:
            copy.wait()

    def stage(k):
        if k > 0:
            arrived(UP, k, lane)
        pl.when(above)(lambda: up(k).start()) if k < planes - 1 else None
        side(k).start()
        pair(k).start()

    def forward(k):
        arrived(SIDE, k, other_lane)
        diagonal(k).start()

    for k in range(planes):
        pl.when(plane >= k)(functools.partial(stage, k))
        if k == 0:

            @pl.when(has_later)
            def _():
                window(0).start()
                window(1).start()

        else:
            pl.when(plane >= k - 1)(functools.partial(forward, k - 1))
    pl.when(plane >= planes - 1)(functools.partial(forward, planes - 1))

    def finish(k):
        arrived(PAIRED, k, twin_lane)
        arrived(DIAGONAL, k, lax.rem(twin_lane + 2, LANES))
        side(k).wait_send()
        pair(k).wait_send()
        diagonal(k).wait_send()
        if k < planes - 1:
            pl.when(above)(lambda: up(k).wait_send())

    for k in range(planes):
        pl.when(plane >= k)(functools.partial(finish, k))
    own.wait()

    @pl.when(has_earlier)
    def _():
        window(0).wait_recv()
        window(1).wait_recv()

    @pl.when(has_later)
    def _():
        window(0).wait_send()
        window(1).wait_send()


def gather(picked, keys, values):
    shard_count = lax.axis_size("ctx")
    planes = shard_count // LANES
    kv_heads = keys.shape[1] // HD
    whole = pl.BlockSpec(memory_space=pltpu.VMEM)
    anywhere = pl.BlockSpec(memory_space=pl.ANY)
    block = (kv_heads, CAP * BLK, 2 * HD)
    return pl.pallas_call(
        functools.partial(gather_kernel, shard_count),
        out_shape=[
            jax.ShapeDtypeStruct((shard_count,) + block, keys.dtype),
            jax.ShapeDtypeStruct(keys.shape, keys.dtype),
            jax.ShapeDtypeStruct(values.shape, values.dtype),
        ],
        in_specs=[pl.BlockSpec(memory_space=pltpu.SMEM), whole, whole],
        out_specs=[anywhere, anywhere, anywhere],
        scratch_shapes=[
            pltpu.VMEM(block, keys.dtype),
            pltpu.SemaphoreType.DMA((4, planes)),
            pltpu.SemaphoreType.DMA((4, planes)),
            pltpu.SemaphoreType.DMA((2,)),
            pltpu.SemaphoreType.DMA((2,)),
            pltpu.SemaphoreType.DMA((3,)),
        ],
        compiler_params=pltpu.CompilerParams(collective_id=0, has_side_effects=True),
    )(picked.reshape(-1), keys, values)


def attend_kernel(
    first, chunks, group_size,
    columns_ref, rank_ref, query_ref, band_ref, pool_ref,
    earlier_keys_ref, keys_ref, earlier_values_ref, values_ref, weight_ref,
    out_ref, away_ref,
    attended, away_weight, weight_sem, window_k, window_v, far_k, far_v, far_s, near_s, far_p, near_p,
):
    step = pl.program_id(0)
    shard = lax.axis_index("ctx")
    kv_heads = window_k.shape[0]
    block_count = pool_ref.shape[0] * WB
    half = away_weight.shape[1]
    away_lanes = pl.ds(pl.multiple_of((1 - lax.axis_index("kvh")) * half, HD), half)
    weight_copy = pltpu.make_async_copy(weight_ref.at[:, away_lanes], away_weight, weight_sem)

    @pl.when(step == 0)
    def _():
        weight_copy.start()
        ones = jnp.ones((2 * WIN, HD), jnp.bfloat16)
        for kv in range(kv_heads):
            lanes = slice(kv * HD, (kv + 1) * HD)
            window_k[kv, :WIN] = earlier_keys_ref[:, lanes]
            window_k[kv, WIN:] = keys_ref[:, lanes]
            window_v[kv, :WIN, :HD] = earlier_values_ref[:, lanes]
            window_v[kv, WIN:, :HD] = values_ref[:, lanes]
            window_v[kv, :, HD:] = ones
        for pair in range(PAIR):
            far_v[pair, :, HD:] = jnp.ones((NV * BLK, HD), jnp.bfloat16)

    before = jnp.where(shard == 0, masked_score, 0.0).astype(jnp.float32)
    row_lane = lax.broadcasted_iota(jnp.int32, (BLK, BLK), 0)
    key_lane = lax.broadcasted_iota(jnp.int32, (BLK, BLK), 1)
    lower = row_lane >= key_lane

    tops = []
    for pair in range(PAIR):
        head = step * PAIR + pair
        kv = head // group_size
        query = query_ref[:, pair * HD : (pair + 1) * HD]
        blocks = []
        for n in range(NV):
            block = columns_ref[head * NV + n]
            blocks.append(block)
            source = jnp.minimum(block // WB, shard)
            rank = jnp.minimum(rank_ref[kv * block_count + block], CAP - 1)
            rows = pl.ds(pl.multiple_of(rank * BLK, BLK), BLK)
            far_k[pair, n * BLK : (n + 1) * BLK] = pool_ref[source, kv, rows, :HD]
            far_v[pair, n * BLK : (n + 1) * BLK, :HD] = pool_ref[source, kv, rows, HD:]
        band = pltpu.roll(
            jnp.broadcast_to(band_ref[pair], (BLK, NEAR + BLK)), 0, 1, stride=1, stride_axis=0
        )[:, :NEAR]
        peak = [None] * chunks
        for a in range(chunks):
            rows = slice(a * BLK, (a + 1) * BLK)
            scores = lax.dot_general(
                query[rows],
                window_k[kv, (first + a) * BLK : (first + a) * BLK + NEAR],
                (((1,), (1,)), ((), ())),
                preferred_element_type=jnp.float32,
            )
            oldest = (shard - 1) * WB + first + a
            hit = blocks[0] == oldest
            for n in range(1, NV):
                hit = hit | (blocks[n] == oldest)
            extra = jnp.where(hit, 0.0, masked_score).astype(jnp.float32)
            for t in range(WB + 1):
                lanes = slice(t * BLK, (t + 1) * BLK)
                mask = band[:, lanes]
                if t == 0:
                    mask = jnp.where(lower, extra, mask)
                if first + a + t < WB:
                    mask = mask + before
                tile = scores[:, lanes] + mask
                near_s[pair, rows, lanes] = tile
                peak[a] = tile if peak[a] is None else jnp.maximum(peak[a], tile)
        wide = 4
        for j in range(NV // wide):
            scores = lax.dot_general(
                query,
                far_k[pair, j * wide * BLK : (j + 1) * wide * BLK],
                (((1,), (1,)), ((), ())),
                preferred_element_type=jnp.float32,
            )
            for a in range(chunks):
                rows = slice(a * BLK, (a + 1) * BLK)
                for t in range(wide):
                    n = j * wide + t
                    old = blocks[n] < (shard - 1) * WB + first + a
                    bias = jnp.where(old, 0.0, masked_score).astype(jnp.float32)
                    tile = scores[rows, t * BLK : (t + 1) * BLK] + bias
                    far_s[pair, rows, n * BLK : (n + 1) * BLK] = tile
                    peak[a] = jnp.maximum(peak[a], tile)
        tops.append([jnp.max(peak[a], axis=1, keepdims=True) for a in range(chunks)])

    for pair in range(PAIR):
        head = step * PAIR + pair
        kv = head // group_size
        for a in range(chunks):
            rows = slice(a * BLK, (a + 1) * BLK)
            top = jnp.broadcast_to(tops[pair][a], (BLK, BLK))
            for t in range(WB + 1):
                lanes = slice(t * BLK, (t + 1) * BLK)
                near_p[pair, rows, lanes] = jnp.exp2(
                    (near_s[pair, rows, lanes] - top) * EXP2_SCALE
                ).astype(jnp.bfloat16)
            for n in range(NV):
                lanes = slice(n * BLK, (n + 1) * BLK)
                far_p[pair, rows, lanes] = jnp.exp2(
                    (far_s[pair, rows, lanes] - top) * EXP2_SCALE
                ).astype(jnp.bfloat16)
        total = jnp.dot(far_p[pair], far_v[pair], preferred_element_type=jnp.float32)
        for a in range(chunks):
            rows = slice(a * BLK, (a + 1) * BLK)
            sums = total[rows] + jnp.dot(
                near_p[pair, rows],
                window_v[kv, (first + a) * BLK : (first + a) * BLK + NEAR],
                preferred_element_type=jnp.float32,
            )
            result = (sums[:, :HD] / sums[:, HD:]).astype(jnp.bfloat16)
            out_ref[rows, pair * HD : (pair + 1) * HD] = result
            attended[rows, pl.ds(pl.multiple_of(head * HD, HD), HD)] = result

    @pl.when(step == pl.num_programs(0) - 1)
    def _():
        weight_copy.wait()
        for start in range(0, half, 2 * HD):
            lanes = slice(start, start + 2 * HD)
            away_ref[:, lanes] = jnp.dot(
                attended[...], away_weight[:, lanes], preferred_element_type=jnp.float32
            ).astype(away_ref.dtype)


def home_kernel(index_ref, *refs):
    count = (len(refs) - 1) // 2
    weight = refs[count][...]
    for part in range(count):
        refs[count + 1 + part][...] = jnp.dot(
            refs[part][...], weight, preferred_element_type=jnp.float32
        )


def project_home(parts, out_weight):
    depth, width = out_weight.shape
    tile = 2 * HD
    tiles = width // 2 // tile
    index = lax.axis_index("kvh").astype(jnp.int32).reshape(1)
    rows = [part.shape[0] for part in parts]
    return pl.pallas_call(
        home_kernel,
        grid_spec=pltpu.PrefetchScalarGridSpec(
            num_scalar_prefetch=1,
            grid=(tiles,),
            in_specs=[pl.BlockSpec((r, depth), lambda j, _: (0, 0)) for r in rows]
            + [pl.BlockSpec((depth, tile), lambda j, index_ref: (0, index_ref[0] * tiles + j))],
            out_specs=[pl.BlockSpec((r, tile), lambda j, _: (0, j)) for r in rows],
        ),
        out_shape=[jax.ShapeDtypeStruct((r, width // 2), jnp.float32) for r in rows],
        compiler_params=pltpu.CompilerParams(vmem_limit_bytes=32 * 1024 * 1024),
        cost_estimate=pl.CostEstimate(
            flops=sum(rows) * depth * width,
            bytes_accessed=depth * width + sum(rows) * (2 * depth + 2 * width),
            transcendentals=0,
        ),
    )(index, *parts, out_weight)


def attend(first, chunks, queries, band, pool, columns, rank, earlier_keys, keys, earlier_values, values, out_weight):
    width = queries.shape[1]
    rows = chunks * BLK
    half = out_weight.shape[1] // 2
    local_heads = width // HD
    kv_heads = keys.shape[1] // HD
    whole = pl.BlockSpec(memory_space=pltpu.VMEM)
    return pl.pallas_call(
        functools.partial(attend_kernel, first, chunks, local_heads // kv_heads),
        grid_spec=pltpu.PrefetchScalarGridSpec(
            num_scalar_prefetch=2,
            grid=(local_heads // PAIR,),
            in_specs=[
                pl.BlockSpec((rows, PAIR * HD), lambda k, *_: (first // chunks, k)),
                pl.BlockSpec((PAIR, 1, NEAR + BLK), lambda k, *_: (k, 0, 0)),
                whole, whole, whole, whole, whole,
                pl.BlockSpec(memory_space=pl.ANY),
            ],
            out_specs=[
                pl.BlockSpec((rows, PAIR * HD), lambda k, *_: (0, k)),
                pl.BlockSpec((rows, half), lambda k, *_: (0, 0)),
            ],
            scratch_shapes=[
                pltpu.VMEM((rows, width), jnp.bfloat16),
                pltpu.VMEM((width, half), jnp.bfloat16),
                pltpu.SemaphoreType.DMA,
                pltpu.VMEM((kv_heads, 2 * WIN, HD), jnp.bfloat16),
                pltpu.VMEM((kv_heads, 2 * WIN, 2 * HD), jnp.bfloat16),
                pltpu.VMEM((PAIR, NV * BLK, HD), jnp.bfloat16),
                pltpu.VMEM((PAIR, NV * BLK, 2 * HD), jnp.bfloat16),
                pltpu.VMEM((PAIR, rows, NV * BLK), jnp.float32),
                pltpu.VMEM((PAIR, rows, NEAR), jnp.float32),
                pltpu.VMEM((PAIR, rows, NV * BLK), jnp.bfloat16),
                pltpu.VMEM((PAIR, rows, NEAR), jnp.bfloat16),
            ],
        ),
        out_shape=[
            jax.ShapeDtypeStruct((rows, width), jnp.bfloat16),
            jax.ShapeDtypeStruct((rows, half), jnp.bfloat16),
        ],
        compiler_params=pltpu.CompilerParams(vmem_limit_bytes=56 * 1024 * 1024),
        cost_estimate=pl.CostEstimate(
            flops=4 * rows * (NV * BLK + NEAR) * width,
            bytes_accessed=2 * pool.size + 4 * rows * width,
            transcendentals=rows * (NV * BLK + NEAR) * local_heads,
        ),
    )(columns.reshape(-1), rank.reshape(-1), queries, band, pool,
      earlier_keys, keys, earlier_values, values, out_weight)


def shards(queries, keys, values, columns, offsets, out_weight):
    shard_rows = queries.shape[0]
    kv_heads = keys.shape[1] // HD
    owned = shard_rows // BLK
    shard_count = lax.axis_size("ctx")
    shard_index = lax.axis_index("ctx")

    block_lane = jnp.arange(shard_count * owned, dtype=jnp.int32)
    listed = jnp.any(
        columns.reshape(kv_heads, -1)[:, :, None] == block_lane[None, None, :], axis=1
    ).astype(jnp.int32).reshape(kv_heads, shard_count, owned)
    earlier = jnp.arange(owned)[:, None] < jnp.arange(owned)[None, :]
    rank = jnp.sum(listed[:, :, :, None] * earlier[None, None].astype(jnp.int32), axis=2)
    own_listed = lax.dynamic_index_in_dim(listed, shard_index, 1, keepdims=False)
    own_rank = lax.dynamic_index_in_dim(rank, shard_index, 1, keepdims=False)
    slot_lane = jnp.arange(CAP, dtype=jnp.int32)
    chosen = (own_listed[:, None, :] > 0) & (own_rank[:, None, :] == slot_lane[None, :, None])
    picked = jnp.sum(
        jnp.where(chosen, jnp.arange(owned, dtype=jnp.int32)[None, None, :], 0), axis=2
    )
    pool, earlier_keys, earlier_values = gather(picked, keys, values)

    distance = WIN - jnp.arange(NEAR + BLK, dtype=jnp.int32)
    band = jnp.where(
        jnp.any(offsets[:, :, None] == distance[None, None, :], axis=1), 0.0, masked_score
    ).astype(jnp.float32)[:, None, :]

    first = 0
    parts, arrivals = [], []
    for chunks in PARTS:
        attended, away = attend(
            first, chunks, queries, band, pool, columns, rank,
            earlier_keys, keys, earlier_values, values, out_weight,
        )
        parts.append(attended)
        arrivals.append(lax.ppermute(away, "kvh", [(0, 1), (1, 0)]))
        first += chunks
    home = project_home(parts, out_weight)
    return jnp.concatenate(
        [(own + far.astype(jnp.float32)).astype(jnp.bfloat16) for own, far in zip(home, arrivals)],
        axis=0,
    )


def solution(mesh):
    placed = (
        P("ctx", "kvh"),
        P("ctx", "kvh"),
        P("ctx", "kvh"),
        P("kvh", None),
        P("kvh", None),
        P("kvh", None),
    )
    return jax.shard_map(
        shards, mesh=mesh, in_specs=placed, out_specs=P("ctx", "kvh"), check_vma=False
    )
```

```python
import functools
import math

import jax
import jax.numpy as jnp
from jax import lax
from jax.experimental import pallas as pl
from jax.experimental.pallas import tpu as pltpu
from jax.sharding import PartitionSpec as P

HD = 128
BLK = 128
NV = 16
CAP = 2
WIN = 512
WB = WIN // BLK
NEAR = WIN + BLK
PARTS = (2, 2)
LANES = 4
UP, SIDE, PAIRED, DIAGONAL = range(4)
PAIR = 2
EXP2_SCALE = math.log2(math.e) / math.sqrt(HD)

masked_score = -1e30


def gather_kernel(
    shard_count, picked_ref, keys_ref, values_ref,
    pool_ref, earlier_keys_ref, earlier_values_ref,
    packed, send, recv, window_send, window_recv, local,
):
    planes = shard_count // LANES
    me = lax.axis_index("ctx")
    plane, lane = lax.div(me, LANES), lax.rem(me, LANES)
    other_lane = lax.rem(lane + 2, LANES)
    across = plane * LANES + other_lane
    twin = me + 1 - 2 * lax.rem(me, 2)
    mesh_id = pl.DeviceIdType.MESH
    below, above = plane > 0, plane < planes - 1
    has_earlier, has_later = me > 0, me < shard_count - 1

    barrier = pltpu.get_barrier_semaphore()

    def greet(to):
        pl.semaphore_signal(barrier, inc=1, device_id={"ctx": to}, device_id_type=mesh_id)

    greet(across)
    greet(twin)
    beyond = me - 1 + 2 * lax.rem(me, 2)
    has_beyond = (beyond >= 0) & (beyond < shard_count)
    for there, to in ((below, me - LANES), (above, me + LANES), (has_beyond, beyond)):
        pl.when(there)(functools.partial(greet, to))
    kv_heads = packed.shape[0]
    for kv in range(kv_heads):
        lanes = slice(kv * HD, (kv + 1) * HD)
        for slot in range(CAP):
            chosen = jnp.full((BLK, HD), picked_ref[kv, slot], jnp.int32)
            out = slice(slot * BLK, (slot + 1) * BLK)
            for ref, start in ((keys_ref, 0), (values_ref, HD)):
                tile = ref[:BLK, lanes].astype(jnp.float32)
                for block in range(1, ref.shape[0] // BLK):
                    own_tile = ref[block * BLK : (block + 1) * BLK, lanes].astype(jnp.float32)
                    tile = jnp.where(chosen == block, own_tile, tile)
                packed[kv, out, start : start + HD] = tile.astype(packed.dtype)
    peers = jnp.int32(2)
    for there in (below, above, has_beyond):
        peers = peers + jnp.where(there, 1, 0).astype(jnp.int32)
    pl.semaphore_wait(barrier, peers)

    def move(kind, k, slot, to, arrival):
        source = packed if k == 0 and kind != DIAGONAL else pool_ref.at[slot]
        return pltpu.make_async_remote_copy(
            src_ref=source, dst_ref=pool_ref.at[slot],
            send_sem=send.at[kind, k], recv_sem=recv.at[kind, arrival],
            device_id={"ctx": to}, device_id_type=mesh_id,
        )

    def up(k):
        return move(UP, k, (plane - k) * LANES + lane, me + LANES, k + 1)

    def side(k):
        return move(SIDE, k, (plane - k) * LANES + lane, across, k)

    def pair(k):
        return move(PAIRED, k, (plane - k) * LANES + lane, twin, k)

    def diagonal(k):
        return move(DIAGONAL, k, (plane - k) * LANES + other_lane, twin, k)

    def window(i):
        source, target = ((keys_ref, earlier_keys_ref), (values_ref, earlier_values_ref))[i]
        return pltpu.make_async_remote_copy(
            src_ref=source, dst_ref=target,
            send_sem=window_send.at[i], recv_sem=window_recv.at[i],
            device_id={"ctx": me + 1}, device_id_type=mesh_id,
        )

    def arrived(kind, k, from_lane):
        slot = (plane - k) * LANES + from_lane
        pltpu.make_async_remote_copy(
            src_ref=packed, dst_ref=pool_ref.at[slot],
            send_sem=send.at[kind, k], recv_sem=recv.at[kind, k],
            device_id={"ctx": twin}, device_id_type=mesh_id,
        ).wait_recv()

    twin_lane = lane + 1 - 2 * lax.rem(me, 2)
    own = pltpu.make_async_copy(packed, pool_ref.at[me], local.at[0])
    own.start()

    fill = [
        pltpu.make_async_copy(keys_ref, earlier_keys_ref, local.at[1]),
        pltpu.make_async_copy(values_ref, earlier_values_ref, local.at[2]),
    ]

    @pl.when(jnp.logical_not(has_earlier))
    def _():
        for copy in fill:
            copy.start()
        for copy in fill:
            copy.wait()

    def stage(k):
        if k > 0:
            arrived(UP, k, lane)
        pl.when(above)(lambda: up(k).start()) if k < planes - 1 else None
        side(k).start()
        pair(k).start()

    def forward(k):
        arrived(SIDE, k, other_lane)
        diagonal(k).start()

    for k in range(planes):
        pl.when(plane >= k)(functools.partial(stage, k))
        if k == 0:

            @pl.when(has_later)
            def _():
                window(0).start()
                window(1).start()

        else:
            pl.when(plane >= k - 1)(functools.partial(forward, k - 1))
    pl.when(plane >= planes - 1)(functools.partial(forward, planes - 1))

    def finish(k):
        arrived(PAIRED, k, twin_lane)
        arrived(DIAGONAL, k, lax.rem(twin_lane + 2, LANES))
        side(k).wait_send()
        pair(k).wait_send()
        diagonal(k).wait_send()
        if k < planes - 1:
            pl.when(above)(lambda: up(k).wait_send())

    for k in range(planes):
        pl.when(plane >= k)(functools.partial(finish, k))
    own.wait()

    @pl.when(has_earlier)
    def _():
        window(0).wait_recv()
        window(1).wait_recv()

    @pl.when(has_later)
    def _():
        window(0).wait_send()
        window(1).wait_send()


def gather(picked, keys, values):
    shard_count = lax.axis_size("ctx")
    planes = shard_count // LANES
    kv_heads = keys.shape[1] // HD
    whole = pl.BlockSpec(memory_space=pltpu.VMEM)
    anywhere = pl.BlockSpec(memory_space=pl.ANY)
    block = (kv_heads, CAP * BLK, 2 * HD)
    return pl.pallas_call(
        functools.partial(gather_kernel, shard_count),
        out_shape=[
            jax.ShapeDtypeStruct((shard_count,) + block, keys.dtype),
            jax.ShapeDtypeStruct(keys.shape, keys.dtype),
            jax.ShapeDtypeStruct(values.shape, values.dtype),
        ],
        in_specs=[pl.BlockSpec(memory_space=pltpu.SMEM), whole, whole],
        out_specs=[anywhere, anywhere, anywhere],
        scratch_shapes=[
            pltpu.VMEM(block, keys.dtype),
            pltpu.SemaphoreType.DMA((4, planes)),
            pltpu.SemaphoreType.DMA((4, planes)),
            pltpu.SemaphoreType.DMA((2,)),
            pltpu.SemaphoreType.DMA((2,)),
            pltpu.SemaphoreType.DMA((3,)),
        ],
        compiler_params=pltpu.CompilerParams(collective_id=0, has_side_effects=True),
    )(picked, keys, values)


def attend_kernel(
    first, chunks, group_size,
    columns_ref, rank_ref, query_ref, band_ref, pool_ref,
    earlier_keys_ref, keys_ref, earlier_values_ref, values_ref, weight_ref,
    out_ref, away_ref,
    attended, away_weight, weight_sem, window_k, window_v, far_k, far_v, far_s, near_s, far_p, near_p,
):
    step = pl.program_id(0)
    shard = lax.axis_index("ctx")
    kv_heads = window_k.shape[0]
    half = away_weight.shape[1]
    away_lanes = pl.ds(pl.multiple_of((1 - lax.axis_index("kvh")) * half, HD), half)
    weight_copy = pltpu.make_async_copy(weight_ref.at[:, away_lanes], away_weight, weight_sem)

    @pl.when(step == 0)
    def _():
        weight_copy.start()
        ones = jnp.ones((2 * WIN, HD), jnp.bfloat16)
        for kv in range(kv_heads):
            lanes = slice(kv * HD, (kv + 1) * HD)
            window_k[kv, :WIN] = earlier_keys_ref[:, lanes]
            window_k[kv, WIN:] = keys_ref[:, lanes]
            window_v[kv, :WIN, :HD] = earlier_values_ref[:, lanes]
            window_v[kv, WIN:, :HD] = values_ref[:, lanes]
            window_v[kv, :, HD:] = ones
        for pair in range(PAIR):
            far_v[pair, :, HD:] = jnp.ones((NV * BLK, HD), jnp.bfloat16)

    before = jnp.where(shard == 0, masked_score, 0.0).astype(jnp.float32)
    row_lane = lax.broadcasted_iota(jnp.int32, (BLK, BLK), 0)
    key_lane = lax.broadcasted_iota(jnp.int32, (BLK, BLK), 1)
    lower = row_lane >= key_lane

    tops = []
    for pair in range(PAIR):
        head = step * PAIR + pair
        kv = head // group_size
        query = query_ref[:, pair * HD : (pair + 1) * HD]
        blocks = []
        for n in range(NV):
            block = columns_ref[head, n]
            blocks.append(block)
            source = jnp.minimum(block // WB, shard)
            rank = jnp.minimum(rank_ref[kv, block], CAP - 1)
            rows = pl.ds(pl.multiple_of(rank * BLK, BLK), BLK)
            far_k[pair, n * BLK : (n + 1) * BLK] = pool_ref[source, kv, rows, :HD]
            far_v[pair, n * BLK : (n + 1) * BLK, :HD] = pool_ref[source, kv, rows, HD:]
        band = pltpu.roll(
            jnp.broadcast_to(band_ref[pair], (BLK, NEAR + BLK)), 0, 1, stride=1, stride_axis=0
        )[:, :NEAR]
        peak = [None] * chunks
        for a in range(chunks):
            rows = slice(a * BLK, (a + 1) * BLK)
            scores = lax.dot_general(
                query[rows],
                window_k[kv, (first + a) * BLK : (first + a) * BLK + NEAR],
                (((1,), (1,)), ((), ())),
                preferred_element_type=jnp.float32,
            )
            oldest = (shard - 1) * WB + first + a
            hit = blocks[0] == oldest
            for n in range(1, NV):
                hit = hit | (blocks[n] == oldest)
            extra = jnp.where(hit, 0.0, masked_score).astype(jnp.float32)
            for t in range(WB + 1):
                lanes = slice(t * BLK, (t + 1) * BLK)
                mask = band[:, lanes]
                if t == 0:
                    mask = jnp.where(lower, extra, mask)
                if first + a + t < WB:
                    mask = mask + before
                tile = scores[:, lanes] + mask
                near_s[pair, rows, lanes] = tile
                peak[a] = tile if peak[a] is None else jnp.maximum(peak[a], tile)
        wide = 4
        for j in range(NV // wide):
            scores = lax.dot_general(
                query,
                far_k[pair, j * wide * BLK : (j + 1) * wide * BLK],
                (((1,), (1,)), ((), ())),
                preferred_element_type=jnp.float32,
            )
            for a in range(chunks):
                rows = slice(a * BLK, (a + 1) * BLK)
                for t in range(wide):
                    n = j * wide + t
                    old = blocks[n] < (shard - 1) * WB + first + a
                    bias = jnp.where(old, 0.0, masked_score).astype(jnp.float32)
                    tile = scores[rows, t * BLK : (t + 1) * BLK] + bias
                    far_s[pair, rows, n * BLK : (n + 1) * BLK] = tile
                    peak[a] = jnp.maximum(peak[a], tile)
        tops.append([jnp.max(peak[a], axis=1, keepdims=True) for a in range(chunks)])

    for pair in range(PAIR):
        head = step * PAIR + pair
        kv = head // group_size
        for a in range(chunks):
            rows = slice(a * BLK, (a + 1) * BLK)
            top = jnp.broadcast_to(tops[pair][a], (BLK, BLK))
            for t in range(WB + 1):
                lanes = slice(t * BLK, (t + 1) * BLK)
                near_p[pair, rows, lanes] = jnp.exp2(
                    (near_s[pair, rows, lanes] - top) * EXP2_SCALE
                ).astype(jnp.bfloat16)
            for n in range(NV):
                lanes = slice(n * BLK, (n + 1) * BLK)
                far_p[pair, rows, lanes] = jnp.exp2(
                    (far_s[pair, rows, lanes] - top) * EXP2_SCALE
                ).astype(jnp.bfloat16)
        total = jnp.dot(far_p[pair], far_v[pair], preferred_element_type=jnp.float32)
        for a in range(chunks):
            rows = slice(a * BLK, (a + 1) * BLK)
            sums = total[rows] + jnp.dot(
                near_p[pair, rows],
                window_v[kv, (first + a) * BLK : (first + a) * BLK + NEAR],
                preferred_element_type=jnp.float32,
            )
            result = (sums[:, :HD] / sums[:, HD:]).astype(jnp.bfloat16)
            out_ref[rows, pair * HD : (pair + 1) * HD] = result
            attended[rows, pl.ds(pl.multiple_of(head * HD, HD), HD)] = result

    @pl.when(step == pl.num_programs(0) - 1)
    def _():
        weight_copy.wait()
        for start in range(0, half, 2 * HD):
            lanes = slice(start, start + 2 * HD)
            away_ref[:, lanes] = jnp.dot(
                attended[...], away_weight[:, lanes], preferred_element_type=jnp.float32
            ).astype(away_ref.dtype)


def home_kernel(index_ref, *refs):
    count = (len(refs) - 1) // 2
    weight = refs[count][...]
    for part in range(count):
        refs[count + 1 + part][...] = jnp.dot(
            refs[part][...], weight, preferred_element_type=jnp.float32
        )


def project_home(parts, out_weight):
    depth, width = out_weight.shape
    tile = 2 * HD
    tiles = width // 2 // tile
    index = lax.axis_index("kvh").astype(jnp.int32).reshape(1)
    rows = [part.shape[0] for part in parts]
    return pl.pallas_call(
        home_kernel,
        grid_spec=pltpu.PrefetchScalarGridSpec(
            num_scalar_prefetch=1,
            grid=(tiles,),
            in_specs=[pl.BlockSpec((r, depth), lambda j, _: (0, 0)) for r in rows]
            + [pl.BlockSpec((depth, tile), lambda j, index_ref: (0, index_ref[0] * tiles + j))],
            out_specs=[pl.BlockSpec((r, tile), lambda j, _: (0, j)) for r in rows],
        ),
        out_shape=[jax.ShapeDtypeStruct((r, width // 2), jnp.float32) for r in rows],
        compiler_params=pltpu.CompilerParams(vmem_limit_bytes=32 * 1024 * 1024),
        cost_estimate=pl.CostEstimate(
            flops=sum(rows) * depth * width,
            bytes_accessed=depth * width + sum(rows) * (2 * depth + 2 * width),
            transcendentals=0,
        ),
    )(index, *parts, out_weight)


def attend(first, chunks, queries, band, pool, columns, rank, earlier_keys, keys, earlier_values, values, out_weight):
    width = queries.shape[1]
    rows = chunks * BLK
    half = out_weight.shape[1] // 2
    local_heads = width // HD
    kv_heads = keys.shape[1] // HD
    whole = pl.BlockSpec(memory_space=pltpu.VMEM)
    return pl.pallas_call(
        functools.partial(attend_kernel, first, chunks, local_heads // kv_heads),
        grid_spec=pltpu.PrefetchScalarGridSpec(
            num_scalar_prefetch=2,
            grid=(local_heads // PAIR,),
            in_specs=[
                pl.BlockSpec((rows, PAIR * HD), lambda k, *_: (first // chunks, k)),
                pl.BlockSpec((PAIR, 1, NEAR + BLK), lambda k, *_: (k, 0, 0)),
                whole, whole, whole, whole, whole,
                pl.BlockSpec(memory_space=pl.ANY),
            ],
            out_specs=[
                pl.BlockSpec((rows, PAIR * HD), lambda k, *_: (0, k)),
                pl.BlockSpec((rows, half), lambda k, *_: (0, 0)),
            ],
            scratch_shapes=[
                pltpu.VMEM((rows, width), jnp.bfloat16),
                pltpu.VMEM((width, half), jnp.bfloat16),
                pltpu.SemaphoreType.DMA,
                pltpu.VMEM((kv_heads, 2 * WIN, HD), jnp.bfloat16),
                pltpu.VMEM((kv_heads, 2 * WIN, 2 * HD), jnp.bfloat16),
                pltpu.VMEM((PAIR, NV * BLK, HD), jnp.bfloat16),
                pltpu.VMEM((PAIR, NV * BLK, 2 * HD), jnp.bfloat16),
                pltpu.VMEM((PAIR, rows, NV * BLK), jnp.float32),
                pltpu.VMEM((PAIR, rows, NEAR), jnp.float32),
                pltpu.VMEM((PAIR, rows, NV * BLK), jnp.bfloat16),
                pltpu.VMEM((PAIR, rows, NEAR), jnp.bfloat16),
            ],
        ),
        out_shape=[
            jax.ShapeDtypeStruct((rows, width), jnp.bfloat16),
            jax.ShapeDtypeStruct((rows, half), jnp.bfloat16),
        ],
        compiler_params=pltpu.CompilerParams(vmem_limit_bytes=56 * 1024 * 1024),
        cost_estimate=pl.CostEstimate(
            flops=4 * rows * (NV * BLK + NEAR) * width,
            bytes_accessed=2 * pool.size + 4 * rows * width,
            transcendentals=rows * (NV * BLK + NEAR) * local_heads,
        ),
    )(columns, rank.reshape(kv_heads, -1), queries, band, pool,
      earlier_keys, keys, earlier_values, values, out_weight)


def shards(queries, keys, values, columns, offsets, out_weight):
    shard_rows = queries.shape[0]
    kv_heads = keys.shape[1] // HD
    owned = shard_rows // BLK
    shard_count = lax.axis_size("ctx")
    shard_index = lax.axis_index("ctx")

    block_lane = jnp.arange(shard_count * owned, dtype=jnp.int32)
    listed = jnp.any(
        columns.reshape(kv_heads, -1)[:, :, None] == block_lane[None, None, :], axis=1
    ).astype(jnp.int32).reshape(kv_heads, shard_count, owned)
    earlier = jnp.arange(owned)[:, None] < jnp.arange(owned)[None, :]
    rank = jnp.sum(listed[:, :, :, None] * earlier[None, None].astype(jnp.int32), axis=2)
    own_listed = lax.dynamic_index_in_dim(listed, shard_index, 1, keepdims=False)
    own_rank = lax.dynamic_index_in_dim(rank, shard_index, 1, keepdims=False)
    slot_lane = jnp.arange(CAP, dtype=jnp.int32)
    chosen = (own_listed[:, None, :] > 0) & (own_rank[:, None, :] == slot_lane[None, :, None])
    picked = jnp.sum(
        jnp.where(chosen, jnp.arange(owned, dtype=jnp.int32)[None, None, :], 0), axis=2
    )
    pool, earlier_keys, earlier_values = gather(picked, keys, values)

    distance = WIN - jnp.arange(NEAR + BLK, dtype=jnp.int32)
    band = jnp.where(
        jnp.any(offsets[:, :, None] == distance[None, None, :], axis=1), 0.0, masked_score
    ).astype(jnp.float32)[:, None, :]

    first = 0
    parts, arrivals = [], []
    for chunks in PARTS:
        attended, away = attend(
            first, chunks, queries, band, pool, columns, rank,
            earlier_keys, keys, earlier_values, values, out_weight,
        )
        parts.append(attended)
        arrivals.append(lax.ppermute(away, "kvh", [(0, 1), (1, 0)]))
        first += chunks
    home = project_home(parts, out_weight)
    return jnp.concatenate(
        [(own + far.astype(jnp.float32)).astype(jnp.bfloat16) for own, far in zip(home, arrivals)],
        axis=0,
    )


def solution(mesh):
    placed = (
        P("ctx", "kvh"),
        P("ctx", "kvh"),
        P("ctx", "kvh"),
        P("kvh", None),
        P("kvh", None),
        P("kvh", None),
    )
    return jax.shard_map(
        shards, mesh=mesh, in_specs=placed, out_specs=P("ctx", "kvh"), check_vma=False
    )
```
